32 devices in a mesh: tex: 4 (over x, core), smp: 8 (over z, y).
Axes of the slice: x: 2, y: 2, z: 4, core: 2. Of those that a mesh axis runs over, the one named last changes fastest.
Arguments:
- blocks: int32 [4, 8, 2, 2], P('tex', 'smp'), may hold values from -1 to 3, as said below
- observed: float32 [4, 8, 512, 256], P('tex', 'smp'), may hold values from 0.05 to 1.5
- w_factor: float32 [64, 4096], P('smp', 'tex'), may hold values from 0.03 to 0.5
- h_factor: float32 [64, 8192], P('tex', 'smp'), may hold values from 0.03 to 0.5
Outputs:
- w_final: float32 [64, 4096], P('smp', 'tex')
- h_final: float32 [64, 8192], P('tex', 'smp')
The draws below stay inside these ranges and needn't reach their ends.
Inputs may be any that keep to these rules, and one draw needn't show every extreme that they name: blocks[t, s, 0, j] is a block row (below 4) and blocks[t, s, 1, j] a block column (below 4) of device (t, s)'s tile, or both are -1 for an empty slot; live slots come first and name different blocks; each device has at least one live slot and some device has 2; every block row of texels is observed on some device along smp, and every block column of samples on some device along tex.
All inputs are finite; a program needn't handle non-finite values.
Results may differ from the reference program's by a relative error of at most 0.0003.
Values sent between devices are 32-bit elements; how exact they have to be, the bound alone decides.
A program may use at most 64 MiB of HBM per device.

```python
import math
import jax
import jax.numpy as jnp
from jax import lax

K = 64
BS = 256
RB = 4
CB = 4
CAP = 2
ITERS = 2
M = 4096
N = 8192
N_TEX = 4
N_SMP = 8


def draw_blocks(key, part):
    key_count = jax.random.fold_in(key, 11)
    key_score = jax.random.fold_in(key, 12)
    key_full = jax.random.fold_in(key, 13)
    devices_all = N_TEX * N_SMP
    tile_blocks = RB * CB
    counts = jax.random.randint(key_count, (N_TEX, N_SMP), max(1, CAP // 4), CAP + 1)
    full_at = jax.random.randint(key_full, (), 0, devices_all)
    counts = jnp.where(jnp.arange(devices_all).reshape(N_TEX, N_SMP) == full_at, CAP, counts)
    scores = jax.random.randint(key_score, (N_TEX, N_SMP, tile_blocks), 0, 1 << 20) * tile_blocks + jnp.arange(tile_blocks)
    texels = jnp.arange(N_TEX)[:, None]
    samples = jnp.arange(N_SMP)[None, :]
    forced = samples % RB * CB + texels % CB
    scores = jnp.where(jnp.arange(tile_blocks)[None, None, :] == forced[:, :, None], -1, scores)
    chosen = jnp.argsort(scores, axis=-1)[:, :, :CAP].astype(jnp.int32)
    live = jnp.arange(CAP)[None, None, :] < counts[:, :, None]
    rows = jnp.where(live, chosen // CB, -1)
    cols = jnp.where(live, chosen % CB, -1)
    return jnp.stack([rows, cols], axis=2).astype(jnp.int32)


def level_of(own_key, extent, pieces, low, largest):
    def one(position, parts):
        steps = jax.random.uniform(jax.random.fold_in(jax.random.fold_in(own_key, 6), position), (parts,), jnp.float32, low / len(pieces), largest / len(pieces))
        return jnp.repeat(jnp.exp(steps), extent[position] // parts).reshape((-1,) + (1,) * (len(extent) - position - 1))

    factor_of = one(*pieces[0])
    for cut in pieces[1:]:
        factor_of = factor_of * one(*cut)
    return factor_of


def setup_inputs(seed: int = 0) -> dict:
    key_list = jax.random.split(jax.random.key(seed), 5)
    blocks = draw_blocks(jax.random.fold_in(key_list[4], 71), 0)
    observed = jnp.clip(0.05 + 1.45 * jax.random.uniform(key_list[1], (N_TEX, N_SMP, CAP * BS, BS), jnp.float32) ** level_of(key_list[1], (N_TEX, N_SMP, CAP * BS, BS), ((0, 4), (1, 8)), -0.2, 0.2), 0.05, 1.5)
    w_factor = jnp.clip(jnp.exp(math.log(0.5) - 2.8134107 * jax.random.uniform(key_list[2], (K, M), jnp.float32) ** level_of(key_list[2], (K, M), ((0, 8), (1, 4)), -0.2, 0.2)), 0.03, 0.5)
    h_factor = jnp.clip(jnp.exp(math.log(0.5) - 2.8134107 * jax.random.uniform(key_list[3], (K, N), jnp.float32) ** level_of(key_list[3], (K, N), ((0, 4), (1, 8)), -0.2, 0.2)), 0.03, 0.5)
    return dict(blocks=blocks, observed=observed, w_factor=w_factor, h_factor=h_factor)


highest = lax.Precision.HIGHEST


def pick_tables(listing, rows_count, cols_count):
    rows = listing[0]
    cols = listing[1]
    live = (rows >= 0).astype(jnp.float32)
    row_pick = (jnp.maximum(rows, 0)[:, None] == jnp.arange(rows_count)[None, :]).astype(jnp.float32) * live[:, None]
    col_pick = (jnp.maximum(cols, 0)[:, None] == jnp.arange(cols_count)[None, :]).astype(jnp.float32)
    return row_pick, col_pick


def block_factors(w_tile, h_tile, row_pick, col_pick):
    rank = w_tile.shape[0]
    w_blocks = jnp.einsum('sr,krb->skb', row_pick, w_tile.reshape(rank, row_pick.shape[1], -1), precision=highest)
    h_blocks = jnp.einsum('sc,kcb->skb', col_pick, h_tile.reshape(rank, col_pick.shape[1], -1), precision=highest)
    approx = jnp.einsum('ska,skb->sab', w_blocks, h_blocks, precision=highest)
    return w_blocks, h_blocks, approx


def basis_terms(w_tile, h_tile, row_pick, col_pick, values):
    w_blocks, h_blocks, approx = block_factors(w_tile, h_tile, row_pick, col_pick)
    upper = jnp.einsum('ska,sab->skb', w_blocks, values, precision=highest)
    lower = jnp.einsum('ska,sab->skb', w_blocks, approx, precision=highest)
    upper = jnp.einsum('sc,skb->kcb', col_pick, upper, precision=highest)
    lower = jnp.einsum('sc,skb->kcb', col_pick, lower, precision=highest)
    return upper.reshape(h_tile.shape), lower.reshape(h_tile.shape)


def weight_terms(w_tile, h_tile, row_pick, col_pick, values):
    w_blocks, h_blocks, approx = block_factors(w_tile, h_tile, row_pick, col_pick)
    upper = jnp.einsum('skb,sab->ska', h_blocks, values, precision=highest)
    lower = jnp.einsum('skb,sab->ska', h_blocks, approx, precision=highest)
    upper = jnp.einsum('sr,ska->kra', row_pick, upper, precision=highest)
    lower = jnp.einsum('sr,ska->kra', row_pick, lower, precision=highest)
    return upper.reshape(w_tile.shape), lower.reshape(w_tile.shape)


def reference(blocks, observed, w_factor, h_factor):
    tiles_w = jnp.moveaxis(w_factor.reshape(K, N_TEX, RB * BS), 1, 0)
    tiles_h = jnp.moveaxis(h_factor.reshape(K, N_SMP, CB * BS), 1, 0)
    values_all = observed.reshape(N_TEX, N_SMP, CAP, BS, BS)
    for sweep in range(ITERS):
        def over_tex(carry, inputs):
            w_tile, listing_row, value_row = inputs

            def per_sample(items):
                h_tile, listing, values = items
                row_pick, col_pick = pick_tables(listing, RB, CB)
                return basis_terms(w_tile, h_tile, row_pick, col_pick, values)

            upper, lower = lax.map(per_sample, (tiles_h, listing_row, value_row))
            return (carry[0] + upper, carry[1] + lower), None

        start = jnp.zeros(tiles_h.shape, jnp.float32)
        (upper, lower), _ = lax.scan(over_tex, (start, start), (tiles_w, blocks, values_all))
        tiles_h = tiles_h * upper / lower

        def texel_sums(inputs):
            w_tile, listing_row, value_row = inputs

            def per_sample(items):
                h_tile, listing, values = items
                row_pick, col_pick = pick_tables(listing, RB, CB)
                return weight_terms(w_tile, h_tile, row_pick, col_pick, values)

            upper, lower = lax.map(per_sample, (tiles_h, listing_row, value_row))
            return jnp.sum(upper, axis=0), jnp.sum(lower, axis=0)

        upper, lower = lax.map(texel_sums, (tiles_w, blocks, values_all))
        tiles_w = tiles_w * upper / lower
    w_final = jnp.moveaxis(tiles_w, 0, 1).reshape(K, N_TEX * RB * BS)
    h_final = jnp.moveaxis(tiles_h, 0, 1).reshape(K, N_SMP * CB * BS)
    return w_final, h_final
```

```python
import functools

import jax
import jax.numpy as jnp
from jax import lax
from jax.experimental import pallas as pl
from jax.experimental.pallas import tpu as pltpu
from jax.sharding import PartitionSpec as P

ITERS = 2
MESH = pl.DeviceIdType.MESH
LANES = 128
ROW_ROW = (((1,), (0,)), ((), ()))
LAST_LAST = (((1,), (1,)), ((), ()))


def halves(x):
    high = x.astype(jnp.bfloat16)
    low = (x - high.astype(jnp.float32)).astype(jnp.bfloat16)
    return high, low


def dot3(a, b, dims):
    def one(x, y):
        return lax.dot_general(x, y, dims, preferred_element_type=jnp.float32)

    return one(a[0], b[0]) + (one(a[0], b[1]) + one(a[1], b[0]))


def weight(place, c):
    return (1 - jnp.minimum(jnp.abs(place - c), 1)).astype(jnp.float32)


def put_rows(buf, x, lanes):
    parts, rows, _ = buf.shape
    if rows % 8 == 0:
        buf[:, :, lanes] = x.reshape(parts, rows, x.shape[1])
    else:
        for p in range(parts):
            buf[p, :, lanes] = x[p * rows : (p + 1) * rows]


def get_rows(full, buf):
    parts, rows, _ = buf.shape
    for p in range(parts):
        full[p * rows : (p + 1) * rows, :] = buf[p]


def kernel(
    sizes, listing, values_hbm, w_in, h_in, w_out, h_out,
    values, high, low, note, tex_note, smp_note, tex_list, smp_list,
    w_buf, h_buf, w_full, h_full, h_send, h_recv, w_send, w_recv, h_new, w_new,
    send_t, recv_t, send_s, recv_s, local,
):
    n_tex, n_smp = sizes
    cap, block, _ = values.shape
    rank, texels = w_full.shape[1:]
    samples = h_full.shape[2]
    me_t, me_s = lax.axis_index("tex"), lax.axis_index("smp")
    axes = {
        "tex": (me_t, n_tex, send_t, recv_t),
        "smp": (me_s, n_smp, send_s, recv_s),
    }

    fetch = pltpu.make_async_copy(values_hbm, values, local.at[0])
    fetch.start()

    barrier = pltpu.get_barrier_semaphore()
    for axis, (me, n, _, _) in axes.items():
        for d in range(1, n):
            pl.semaphore_signal(
                barrier, inc=1, device_id={axis: lax.rem(me + d, n)}, device_id_type=MESH
            )

    lane = lax.broadcasted_iota(jnp.int32, (1, LANES), 1)
    text = jnp.full((1, LANES), -1, jnp.int32)
    for side in range(2):
        for j in range(cap):
            text = jnp.where(lane == side * cap + j, listing[side, j], text)
    note[...] = text
    tex_note[me_t] = text
    smp_note[me_s] = text
    w_buf[0, me_s] = w_in[...]
    h_buf[0, me_t] = h_in[...]

    pl.semaphore_wait(barrier, n_tex + n_smp - 2)

    started = []

    def send(axis, phase, source_of, target):
        me, n, send_sem, recv_sem = axes[axis]
        copies = []
        for d in range(1, n):
            to = lax.rem(me + d, n)
            copy = pltpu.make_async_remote_copy(
                src_ref=source_of(to),
                dst_ref=target.at[me],
                send_sem=send_sem.at[phase, d - 1],
                recv_sem=recv_sem.at[phase, d - 1],
                device_id={axis: to},
                device_id_type=MESH,
            )
            copy.start()
            copies.append(copy)
        started.extend(copies)
        return copies

    def arrive(copies):
        for copy in copies:
            copy.wait_recv()

    w_come = send("smp", 0, lambda to: w_in, w_buf.at[0])
    h_come = send("tex", 0, lambda to: h_in, h_buf.at[0])
    notes = send("smp", 1, lambda to: note, smp_note) + send("tex", 1, lambda to: note, tex_note)

    fetch.wait()
    for j in range(cap):
        high[j], low[j] = halves(values[j])
    arrive(notes)
    copies = [
        pltpu.make_async_copy(tex_note, tex_list, local.at[1]),
        pltpu.make_async_copy(smp_note, smp_list, local.at[2]),
    ]
    for copy in copies:
        copy.start()
    for copy in copies:
        copy.wait()
    arrive(w_come)
    get_rows(w_full.at[0], w_buf.at[0])

    def slot_terms(full, side, dims, out):
        for j in range(cap):
            part = None
            for c in range(full.shape[1] // block):
                term = weight(listing[side, j], c) * full[:, c * block : (c + 1) * block]
                part = term if part is None else part + term
            part = halves(part)
            put_rows(out, dot3(part, (high[j], low[j]), dims), slice(j * block, (j + 1) * block))
            gram = dot3(part, part, LAST_LAST)
            first = cap * block + j * rank
            put_rows(out, gram, slice(first, first + rank))

    def updated(own, full, recv, lists, side):
        parts = recv.shape[0]
        count = own.shape[1] // block
        new = []
        for c in range(count):
            upper = gram = None
            for p in range(parts):
                for j in range(cap):
                    hit = weight(lists[p, 0, side * cap + j], c)
                    first = cap * block + j * rank
                    u = hit * recv[p, :, j * block : (j + 1) * block]
                    g = hit * recv[p, :, first : first + rank]
                    upper = u if upper is None else upper + u
                    gram = g if gram is None else gram + g
            where = slice(c * block, (c + 1) * block)
            lower = dot3(halves(gram), halves(full[:, where]), ROW_ROW)
            new.append(own[:, where] * upper / lower)
        return jnp.concatenate(new, axis=1)

    h_own, w_own = h_in[...], w_in[...]
    for sweep in range(ITERS):
        phase = 2 + 2 * sweep
        slot_terms(w_full.at[sweep], 0, ROW_ROW, h_send.at[sweep])
        come = send("tex", phase, lambda to: h_send.at[sweep, to], h_recv.at[sweep])
        h_recv[sweep, me_t] = h_send[sweep, me_t]
        if sweep == 0:
            arrive(h_come)
            get_rows(h_full.at[0], h_buf.at[0])
        arrive(come)
        h_own = updated(h_own, h_full.at[sweep], h_recv.at[sweep], tex_list, 1)
        h_new[sweep] = h_own
        come = send("tex", phase + 1, lambda to: h_new.at[sweep], h_buf.at[sweep + 1])
        h_buf[sweep + 1, me_t] = h_own
        arrive(come)
        get_rows(h_full.at[sweep + 1], h_buf.at[sweep + 1])

        slot_terms(h_full.at[sweep + 1], 1, LAST_LAST, w_send.at[sweep])
        come = send("smp", phase, lambda to: w_send.at[sweep, to], w_recv.at[sweep])
        w_recv[sweep, me_s] = w_send[sweep, me_s]
        arrive(come)
        w_own = updated(w_own, w_full.at[sweep], w_recv.at[sweep], smp_list, 0)
        if sweep < ITERS - 1:
            w_new[sweep] = w_own
            come = send("smp", phase + 1, lambda to: w_new.at[sweep], w_buf.at[sweep + 1])
            w_buf[sweep + 1, me_s] = w_own
            arrive(come)
            get_rows(w_full.at[sweep + 1], w_buf.at[sweep + 1])
    h_out[...] = h_own
    w_out[...] = w_own
    for copy in started:
        copy.wait_send()


def per_device(n_tex, n_smp, blocks, observed, w_factor, h_factor):
    cap = blocks.shape[3]
    block = observed.shape[3]
    w_rows, texels = w_factor.shape
    h_rows, samples = h_factor.shape
    rank = w_rows * n_smp
    wide = cap * block + -(-cap * rank // LANES) * LANES
    phases = 2 + 2 * ITERS
    f32, vmem = jnp.float32, pltpu.VMEM
    dma = pltpu.SemaphoreType.DMA
    return pl.pallas_call(
        functools.partial(kernel, (n_tex, n_smp)),
        out_shape=(
            jax.ShapeDtypeStruct(w_factor.shape, f32),
            jax.ShapeDtypeStruct(h_factor.shape, f32),
        ),
        in_specs=[
            pl.BlockSpec(memory_space=pltpu.SMEM),
            pl.BlockSpec(memory_space=pl.ANY),
            pl.BlockSpec(memory_space=vmem),
            pl.BlockSpec(memory_space=vmem),
        ],
        out_specs=(pl.BlockSpec(memory_space=vmem),) * 2,
        scratch_shapes=[
            vmem((cap, block, block), f32),
            vmem((cap, block, block), jnp.bfloat16),
            vmem((cap, block, block), jnp.bfloat16),
            vmem((1, LANES), jnp.int32),
            vmem((n_tex, 1, LANES), jnp.int32),
            vmem((n_smp, 1, LANES), jnp.int32),
            pltpu.SMEM((n_tex, 1, LANES), jnp.int32),
            pltpu.SMEM((n_smp, 1, LANES), jnp.int32),
            vmem((ITERS, n_smp, w_rows, texels), f32),
            vmem((ITERS + 1, n_tex, h_rows, samples), f32),
            vmem((ITERS, rank, texels), f32),
            vmem((ITERS + 1, rank, samples), f32),
            vmem((ITERS, n_tex, h_rows, wide), f32),
            vmem((ITERS, n_tex, h_rows, wide), f32),
            vmem((ITERS, n_smp, w_rows, wide), f32),
            vmem((ITERS, n_smp, w_rows, wide), f32),
            vmem((ITERS, h_rows, samples), f32),
            vmem((ITERS, w_rows, texels), f32),
            dma((phases, n_tex - 1)),
            dma((phases, n_tex - 1)),
            dma((phases, n_smp - 1)),
            dma((phases, n_smp - 1)),
            dma((3,)),
        ],
        compiler_params=pltpu.CompilerParams(
            collective_id=0, has_side_effects=True, vmem_limit_bytes=40 * 2**20
        ),
    )(
        blocks.reshape(blocks.shape[2:]),
        observed.reshape(cap, block, block),
        w_factor,
        h_factor,
    )


def solution(mesh):
    in_specs = (
        P("tex", "smp", None, None),
        P("tex", "smp", None, None),
        P("smp", "tex"),
        P("tex", "smp"),
    )
    out_specs = (P("smp", "tex"), P("tex", "smp"))
    return jax.shard_map(
        functools.partial(per_device, mesh.shape["tex"], mesh.shape["smp"]),
        mesh=mesh,
        in_specs=in_specs,
        out_specs=out_specs,
        check_vma=False,
    )
```

```python
import functools

import jax
import jax.numpy as jnp
from jax import lax
from jax.experimental import pallas as pl
from jax.experimental.pallas import tpu as pltpu
from jax.sharding import PartitionSpec as P

ITERS = 2
MESH = pl.DeviceIdType.MESH
LANES = 128
ROW_ROW = (((1,), (0,)), ((), ()))
LAST_LAST = (((1,), (1,)), ((), ()))


def halves(x):
    high = x.astype(jnp.bfloat16)
    low = (x - high.astype(jnp.float32)).astype(jnp.bfloat16)
    return high, low


def dot(a, b, dims=ROW_ROW):
    return lax.dot_general(a, b, dims, preferred_element_type=jnp.float32)


def weight(place, c):
    return (1 - jnp.minimum(jnp.abs(place - c), 1)).astype(jnp.float32)


def put_rows(buf, x, lanes):
    parts, rows, _ = buf.shape
    if rows % 8 == 0:
        buf[:, :, lanes] = x.reshape(parts, rows, x.shape[1])
    else:
        for p in range(parts):
            buf[p, :, lanes] = x[p * rows : (p + 1) * rows]


def get_rows(full, buf):
    parts, rows, _ = buf.shape
    for p in range(parts):
        full[p * rows : (p + 1) * rows, :] = buf[p]


def kernel(
    sizes, listing_hbm, values_hbm, w_in, h_in, w_out, h_out,
    listing, values, high, low, turned_high, turned_low,
    note, tex_note, smp_note, tex_list, smp_list, tex_hot, smp_hot,
    w_buf, h_buf, w_full, h_full, h_send, h_recv, w_send, w_recv, stack,
    send_t, recv_t, send_s, recv_s, local,
):
    n_tex, n_smp = sizes
    cap, block, _ = values.shape
    rank, texels = w_full.shape
    samples = h_full.shape[1]
    me_t, me_s = lax.axis_index("tex"), lax.axis_index("smp")
    axes = {
        "tex": (me_t, n_tex, send_t, recv_t),
        "smp": (me_s, n_smp, send_s, recv_s),
    }

    fetch = [
        pltpu.make_async_copy(w_in, w_buf.at[0, me_s], local.at[0]),
        pltpu.make_async_copy(h_in, h_buf.at[0, me_t], local.at[1]),
        pltpu.make_async_copy(listing_hbm, listing, local.at[2]),
        pltpu.make_async_copy(values_hbm, values, local.at[3]),
    ]
    for copy in fetch:
        copy.start()

    barrier = pltpu.get_barrier_semaphore()
    for axis, (me, n, _, _) in axes.items():
        for d in range(1, n):
            pl.semaphore_signal(
                barrier, inc=1, device_id={axis: lax.rem(me + d, n)}, device_id_type=MESH
            )
    for copy in fetch[:3]:
        copy.wait()
    lane = lax.broadcasted_iota(jnp.int32, (1, LANES), 1)
    text = jnp.full((1, LANES), -1, jnp.int32)
    for side in range(2):
        for j in range(cap):
            text = jnp.where(lane == side * cap + j, listing[side, j], text)
    note[...] = text
    tex_note[me_t] = text
    smp_note[me_s] = text

    pl.semaphore_wait(barrier, n_tex + n_smp - 2)

    started = []

    def push(axis, phase, at, src, dst, to):
        _, _, send_sem, recv_sem = axes[axis]
        copy = pltpu.make_async_remote_copy(
            src_ref=src,
            dst_ref=dst,
            send_sem=send_sem.at[phase, at],
            recv_sem=recv_sem.at[phase, at],
            device_id={axis: to},
            device_id_type=MESH,
        )
        copy.start()
        started.append(copy)
        return copy

    def scatter(axis, phase, source_of, target):
        me, n, _, _ = axes[axis]
        copies = []
        for d in range(1, n):
            to = lax.rem(me + d, n)
            copies.append(push(axis, phase, d - 1, source_of(to), target, to))
        return copies

    def gather_begin(axis, phase, buf):
        me, n, _, _ = axes[axis]
        mine = buf.at[me]
        copies = []
        for d in range(1, n // 2):
            copies.append(push(axis, phase, d - 1, mine, mine, lax.rem(me + 2 * d, n)))
        mate = me + 1 - 2 * lax.rem(me, 2)
        copies.append(push(axis, phase, n // 2 - 1, mine, mine, mate))
        return copies

    def gather_forward(axis, phase, buf, copies):
        me, n, _, _ = axes[axis]
        mate = me + 1 - 2 * lax.rem(me, 2)
        late = copies[-1:]
        for d in range(1, n // 2):
            copies[d - 1].wait_recv()
            came = buf.at[lax.rem(me + n - 2 * d, n)]
            late.append(push(axis, phase, n // 2 - 1 + d, came, came, mate))
        return late

    def arrive(copies):
        for copy in copies:
            copy.wait_recv()

    w_come = gather_begin("smp", 0, w_buf.at[0])
    h_come = gather_begin("tex", 0, h_buf.at[0])
    notes = scatter("smp", 1, lambda to: note, smp_note.at[me_s])
    notes += scatter("tex", 1, lambda to: note, tex_note.at[me_t])

    h_come = gather_forward("tex", 0, h_buf.at[0], h_come)
    w_come = gather_forward("smp", 0, w_buf.at[0], w_come)
    arrive(notes)
    copies = [
        pltpu.make_async_copy(tex_note, tex_list, local.at[4]),
        pltpu.make_async_copy(smp_note, smp_list, local.at[5]),
    ]
    for copy in copies:
        copy.start()
    fetch[3].wait()
    for j in range(cap):
        high[j], low[j] = halves(values[j])
        turned_high[j], turned_low[j] = halves(values[j].T)
    arrive(w_come)
    get_rows(w_full, w_buf.at[0])

    def slot_terms(full, side, weights, out, send):
        parts = []
        edge = cap * block
        for j in range(cap):
            part = None
            for c in range(full.shape[1] // block):
                term = weight(listing[side, j], c) * full[:, c * block : (c + 1) * block]
                part = term if part is None else part + term
            parts.append(halves(part))
            both = jnp.concatenate(parts[j], axis=0)
            twice = dot(both, weights[0][j])
            upper = twice[:rank] + (twice[rank:] + dot(parts[j][0], weights[1][j]))
            put_rows(out, upper, slice(j * block, (j + 1) * block))
            if j == cap - 2:
                come = send(0, pl.ds(0, edge - block))
        for j in range(cap):
            both = jnp.concatenate(parts[j], axis=0)
            twice = dot(both, parts[j][0], LAST_LAST)
            gram = twice[:rank] + (twice[rank:] + dot(parts[j][0], parts[j][1], LAST_LAST))
            put_rows(out, gram, slice(edge + j * rank, edge + (j + 1) * rank))
        return come + send(1, pl.ds(edge - block, out.shape[2] - edge + block))

    def stack_up(full):
        part = halves(full[...])
        stack[:rank, : full.shape[1]] = part[0]
        stack[rank : 2 * rank, : full.shape[1]] = part[1]
        stack[2 * rank :, : full.shape[1]] = part[0]

    def updated(own, recv, hot):
        parts = recv.shape[0]
        count = own.shape[1] // block
        new = []
        for c in range(count):
            upper = gram = None
            for p in range(parts):
                for j in range(cap):
                    hit = hot[(p * cap + j) * count + c]
                    first = cap * block + j * rank
                    u = hit * recv[p, :, j * block : (j + 1) * block]
                    g = hit * recv[p, :, first : first + rank]
                    upper = u if upper is None else upper + u
                    gram = g if gram is None else gram + g
            where = slice(c * block, (c + 1) * block)
            g_high, g_low = halves(gram)
            lower = dot(jnp.concatenate([g_high, g_high, g_low], axis=1), stack[:, where])
            new.append(own[:, where] * upper / lower)
        return jnp.concatenate(new, axis=1)

    def sender(axis, sweep, out, target):
        me = axes[axis][0]

        def send(half, lanes):
            return scatter(
                axis, 2 + 3 * sweep + half,
                lambda to: out.at[to, :, lanes], target.at[me, :, lanes],
            )

        return send

    h_own, w_own = h_buf[0, me_t], w_buf[0, me_s]
    for sweep in range(ITERS):
        out, target = h_send.at[sweep], h_recv.at[sweep]
        come = slot_terms(w_full, 0, (high, low), out, sender("tex", sweep, out, target))
        h_recv[sweep, me_t] = h_send[sweep, me_t]
        if sweep == 0:
            for copy in copies:
                copy.wait()
            for lists, hot, n, side in ((tex_list, tex_hot, n_tex, 1), (smp_list, smp_hot, n_smp, 0)):
                count = (texels, samples)[side] // block
                for p in range(n):
                    for j in range(cap):
                        for c in range(count):
                            hot[(p * cap + j) * count + c] = weight(lists[p, 0, side * cap + j], c)
            arrive(h_come)
            get_rows(h_full, h_buf.at[0])
        stack_up(h_full)
        arrive(come)
        h_own = updated(h_own, h_recv.at[sweep], tex_hot)
        h_buf[sweep + 1, me_t] = h_own
        buf, phase = h_buf.at[sweep + 1], 4 + 3 * sweep
        come = gather_begin("tex", phase, buf)
        stack_up(w_full)
        arrive(gather_forward("tex", phase, buf, come))
        get_rows(h_full, buf)

        out, target = w_send.at[sweep], w_recv.at[sweep]
        come = slot_terms(
            h_full, 1, (turned_high, turned_low), out, sender("smp", sweep, out, target)
        )
        w_recv[sweep, me_s] = w_send[sweep, me_s]
        arrive(come)
        w_own = updated(w_own, w_recv.at[sweep], smp_hot)
        if sweep < ITERS - 1:
            w_buf[sweep + 1, me_s] = w_own
            buf = w_buf.at[sweep + 1]
            come = gather_begin("smp", phase, buf)
            arrive(gather_forward("smp", phase, buf, come))
            get_rows(w_full, buf)
    h_out[...] = h_own
    w_out[...] = w_own
    for copy in started:
        copy.wait_send()


def per_device(n_tex, n_smp, blocks, observed, w_factor, h_factor):
    cap = blocks.shape[3]
    block = observed.shape[3]
    w_rows, texels = w_factor.shape
    h_rows, samples = h_factor.shape
    rank = w_rows * n_smp
    wide = cap * block + -(-cap * rank // LANES) * LANES
    phases = 2 + 3 * ITERS
    f32, half, vmem = jnp.float32, jnp.bfloat16, pltpu.VMEM
    dma = pltpu.SemaphoreType.DMA
    return pl.pallas_call(
        functools.partial(kernel, (n_tex, n_smp)),
        out_shape=(
            jax.ShapeDtypeStruct(w_factor.shape, f32),
            jax.ShapeDtypeStruct(h_factor.shape, f32),
        ),
        in_specs=[pl.BlockSpec(memory_space=pl.ANY)] * 4,
        out_specs=(pl.BlockSpec(memory_space=vmem),) * 2,
        scratch_shapes=[
            pltpu.SMEM(blocks.shape[2:], jnp.int32),
            vmem((cap, block, block), f32),
            vmem((cap, block, block), half),
            vmem((cap, block, block), half),
            vmem((cap, block, block), half),
            vmem((cap, block, block), half),
            vmem((1, LANES), jnp.int32),
            vmem((n_tex, 1, LANES), jnp.int32),
            vmem((n_smp, 1, LANES), jnp.int32),
            pltpu.SMEM((n_tex, 1, LANES), jnp.int32),
            pltpu.SMEM((n_smp, 1, LANES), jnp.int32),
            pltpu.SMEM((n_tex * cap * (samples // block),), f32),
            pltpu.SMEM((n_smp * cap * (texels // block),), f32),
            vmem((ITERS, n_smp, w_rows, texels), f32),
            vmem((ITERS + 1, n_tex, h_rows, samples), f32),
            vmem((rank, texels), f32),
            vmem((rank, samples), f32),
            vmem((ITERS, n_tex, h_rows, wide), f32),
            vmem((ITERS, n_tex, h_rows, wide), f32),
            vmem((ITERS, n_smp, w_rows, wide), f32),
            vmem((ITERS, n_smp, w_rows, wide), f32),
            vmem((3 * rank, max(texels, samples)), half),
            dma((phases, n_tex - 1)),
            dma((phases, n_tex - 1)),
            dma((phases, n_smp - 1)),
            dma((phases, n_smp - 1)),
            dma((6,)),
        ],
        compiler_params=pltpu.CompilerParams(
            collective_id=0, has_side_effects=True, vmem_limit_bytes=60 * 2**20
        ),
    )(
        blocks.reshape(blocks.shape[2:]),
        observed.reshape(cap, block, block),
        w_factor,
        h_factor,
    )


def solution(mesh):
    in_specs = (
        P("tex", "smp", None, None),
        P("tex", "smp", None, None),
        P("smp", "tex"),
        P("tex", "smp"),
    )
    out_specs = (P("smp", "tex"), P("tex", "smp"))
    return jax.shard_map(
        functools.partial(per_device, mesh.shape["tex"], mesh.shape["smp"]),
        mesh=mesh,
        in_specs=in_specs,
        out_specs=out_specs,
        check_vma=False,
    )
```

```python
import functools

import jax
import jax.numpy as jnp
from jax import lax
from jax.experimental import pallas as pl
from jax.experimental.pallas import tpu as pltpu
from jax.sharding import PartitionSpec as P

ITERS = 2
MESH = pl.DeviceIdType.MESH
LANES = 128
ROW_ROW = (((1,), (0,)), ((), ()))
LAST_LAST = (((1,), (1,)), ((), ()))


def halves(x):
    high = x.astype(jnp.bfloat16)
    low = (x - high.astype(jnp.float32)).astype(jnp.bfloat16)
    return high, low


def dot(a, b, dims=ROW_ROW):
    return lax.dot_general(a, b, dims, preferred_element_type=jnp.float32)


def weight(place, c):
    return (1 - jnp.minimum(jnp.abs(place - c), 1)).astype(jnp.float32)


def put_rows(buf, x, lanes):
    parts, rows, _ = buf.shape
    if rows % 8 == 0:
        buf[:, :, lanes] = x.reshape(parts, rows, x.shape[1])
    else:
        for p in range(parts):
            buf[p, :, lanes] = x[p * rows : (p + 1) * rows]


def get_rows(full, buf):
    parts, rows, _ = buf.shape
    for p in range(parts):
        full[p * rows : (p + 1) * rows, :] = buf[p]


def kernel(
    sizes, listing_hbm, values_hbm, w_in, h_in, w_out, h_out,
    listing, values, high, low, turned_high, turned_low,
    note, tex_note, smp_note, tex_list, smp_list, tex_hot, smp_hot,
    w_buf, h_buf, w_full, h_full, h_send, h_recv, w_send, w_recv,
    h_pick, h_picked, w_pick, w_picked, h_part, w_part, h_last, w_last, stack,
    send_t, recv_t, send_s, recv_s, local,
):
    n_tex, n_smp = sizes
    cap, block, _ = values.shape
    rank, texels = w_full.shape
    samples = h_full.shape[1]
    me_t, me_s = lax.axis_index("tex"), lax.axis_index("smp")
    axes = {
        "tex": (me_t, n_tex, send_t, recv_t),
        "smp": (me_s, n_smp, send_s, recv_s),
    }

    fetch = [
        pltpu.make_async_copy(w_in, w_buf.at[0, me_s], local.at[0]),
        pltpu.make_async_copy(h_in, h_buf.at[0, me_t], local.at[1]),
        pltpu.make_async_copy(listing_hbm, listing, local.at[2]),
        pltpu.make_async_copy(values_hbm, values, local.at[3]),
    ]
    for copy in fetch:
        copy.start()

    barrier = pltpu.get_barrier_semaphore()
    for axis, (me, n, _, _) in axes.items():
        for d in range(1, n):
            pl.semaphore_signal(
                barrier, inc=1, device_id={axis: lax.rem(me + d, n)}, device_id_type=MESH
            )
    for copy in fetch[:3]:
        copy.wait()
    lane = lax.broadcasted_iota(jnp.int32, (1, LANES), 1)
    text = jnp.full((1, LANES), -1, jnp.int32)
    for side in range(2):
        for j in range(cap):
            text = jnp.where(lane == side * cap + j, listing[side, j], text)
    note[...] = text
    tex_note[me_t] = text
    smp_note[me_s] = text

    pl.semaphore_wait(barrier, n_tex + n_smp - 2)

    started = []

    def push(axis, phase, at, src, dst, to):
        _, _, send_sem, recv_sem = axes[axis]
        copy = pltpu.make_async_remote_copy(
            src_ref=src,
            dst_ref=dst,
            send_sem=send_sem.at[phase, at],
            recv_sem=recv_sem.at[phase, at],
            device_id={axis: to},
            device_id_type=MESH,
        )
        copy.start()
        started.append(copy)
        return copy

    def scatter(axis, phase, source_of, target):
        me, n, _, _ = axes[axis]
        copies = []
        for d in range(1, n):
            to = lax.rem(me + d, n)
            copies.append(push(axis, phase, d - 1, source_of(to), target, to))
        return copies

    def gather_begin(axis, phase, buf):
        me, n, _, _ = axes[axis]
        mine = buf.at[me]
        copies = []
        for d in range(1, n // 2):
            copies.append(push(axis, phase, d - 1, mine, mine, lax.rem(me + 2 * d, n)))
        mate = me + 1 - 2 * lax.rem(me, 2)
        copies.append(push(axis, phase, n // 2 - 1, mine, mine, mate))
        return copies

    def gather_forward(axis, phase, buf, copies):
        me, n, _, _ = axes[axis]
        mate = me + 1 - 2 * lax.rem(me, 2)
        late = copies[-1:]
        for d in range(1, n // 2):
            copies[d - 1].wait_recv()
            came = buf.at[lax.rem(me + n - 2 * d, n)]
            late.append(push(axis, phase, n // 2 - 1 + d, came, came, mate))
        return late

    def arrive(copies):
        for copy in copies:
            copy.wait_recv()

    w_come = gather_begin("smp", 0, w_buf.at[0])
    h_come = gather_begin("tex", 0, h_buf.at[0])
    notes = scatter("smp", 1, lambda to: note, smp_note.at[me_s])
    notes += scatter("tex", 1, lambda to: note, tex_note.at[me_t])

    h_come = gather_forward("tex", 0, h_buf.at[0], h_come)
    w_come = gather_forward("smp", 0, w_buf.at[0], w_come)
    arrive(notes)
    copies = [
        pltpu.make_async_copy(tex_note, tex_list, local.at[4]),
        pltpu.make_async_copy(smp_note, smp_list, local.at[5]),
    ]
    for copy in copies:
        copy.start()
    fetch[3].wait()
    for j in range(cap):
        high[j], low[j] = halves(values[j])
        turned_high[j], turned_low[j] = halves(values[j].T)
    arrive(w_come)
    get_rows(w_full, w_buf.at[0])

    def part_of_full(full, side, j):
        part = None
        for c in range(full.shape[1] // block):
            term = weight(listing[side, j], c) * full[:, c * block : (c + 1) * block]
            part = term if part is None else part + term
        return part

    def part_of_picked(picked, spare, j):
        where = slice(j * block, (j + 1) * block)
        if picked.shape[1] % 8 == 0:
            return picked[:, :, where].reshape(rank, block)
        if j == 0:
            get_rows(spare, picked)
        return spare[:, where]

    def slot_terms(part_of, weights, out, send):
        parts = []
        edge = cap * block
        for j in range(cap):
            parts.append(halves(part_of(j)))
            both = jnp.concatenate(parts[j], axis=0)
            twice = dot(both, weights[0][j])
            upper = twice[:rank] + (twice[rank:] + dot(parts[j][0], weights[1][j]))
            put_rows(out, upper, slice(j * block, (j + 1) * block))
            if j == cap - 2:
                come = send(0, pl.ds(0, edge - block))
        for j in range(cap):
            both = jnp.concatenate(parts[j], axis=0)
            twice = dot(both, parts[j][0], LAST_LAST)
            gram = twice[:rank] + (twice[rank:] + dot(parts[j][0], parts[j][1], LAST_LAST))
            put_rows(out, gram, slice(edge + j * rank, edge + (j + 1) * rank))
        return come + send(1, pl.ds(edge - block, out.shape[2] - edge + block))

    def stack_up(full):
        part = halves(full[...])
        stack[:rank, : full.shape[1]] = part[0]
        stack[rank : 2 * rank, : full.shape[1]] = part[1]
        stack[2 * rank :, : full.shape[1]] = part[0]

    def updated(axis, own, recv, hot, come):
        me, n, _, _ = axes[axis]
        count = own.shape[1] // block
        upper, gram = [None] * count, [None] * count
        for d in range(n):
            p = lax.rem(me + n - d, n)
            if d > 0:
                arrive([come[d - 1], come[n - 1 + d - 1]])
            for j in range(cap):
                first = cap * block + j * rank
                u = recv[p, :, j * block : (j + 1) * block]
                g = recv[p, :, first : first + rank]
                for c in range(count):
                    hit = hot[(p * cap + j) * count + c]
                    upper[c] = hit * u if upper[c] is None else upper[c] + hit * u
                    gram[c] = hit * g if gram[c] is None else gram[c] + hit * g
        new = []
        for c in range(count):
            where = slice(c * block, (c + 1) * block)
            g_high, g_low = halves(gram[c])
            lower = dot(jnp.concatenate([g_high, g_high, g_low], axis=1), stack[:, where])
            new.append(own[:, where] * upper[c] / lower)
        return jnp.concatenate(new, axis=1)

    def send_picked(axis, phase, new, hot, pick, picked):
        me, n, _, _ = axes[axis]
        count = new.shape[1] // block
        copies = []
        for d in list(range(1, n)) + [0]:
            to = lax.rem(me + d, n)
            for j in range(cap):
                part = None
                for c in range(count):
                    hit = hot[(to * cap + j) * count + c]
                    term = hit * new[:, c * block : (c + 1) * block]
                    part = term if part is None else part + term
                (pick if d else picked)[to, :, j * block : (j + 1) * block] = part
            if d:
                copies.append(push(axis, phase, d - 1, pick.at[to], picked.at[me], to))
        return copies

    def sender(axis, sweep, out, target):
        me = axes[axis][0]

        def send(half, lanes):
            return scatter(
                axis, 2 + 4 * sweep + half,
                lambda to: out.at[to, :, lanes], target.at[me, :, lanes],
            )

        return send

    h_own, w_own = h_buf[0, me_t], w_buf[0, me_s]
    for sweep in range(ITERS):
        phase = 4 + 4 * sweep
        more = sweep < ITERS - 1
        out, target = h_send.at[sweep], h_recv.at[sweep]
        send = sender("tex", sweep, out, target)
        if sweep == 0:
            part_of = functools.partial(part_of_full, w_full, 0)
        else:
            part_of = functools.partial(part_of_picked, w_picked.at[sweep - 1], w_part)
        come = slot_terms(part_of, (high, low), out, send)
        h_recv[sweep, me_t] = h_send[sweep, me_t]
        if sweep == 0:
            for copy in copies:
                copy.wait()
            for lists, hot, n, side in ((tex_list, tex_hot, n_tex, 1), (smp_list, smp_hot, n_smp, 0)):
                count = (texels, samples)[side] // block
                for p in range(n):
                    for j in range(cap):
                        for c in range(count):
                            hot[(p * cap + j) * count + c] = weight(lists[p, 0, side * cap + j], c)
        else:
            mine = w_buf.at[sweep, me_s]
            w_come = scatter("smp", phase + 1, lambda to: mine, mine)
        arrive(h_come)
        get_rows(h_full, h_buf.at[sweep])
        stack_up(h_full)
        h_own = updated("tex", h_own, h_recv.at[sweep], tex_hot, come)
        come = send_picked("tex", phase, h_own, tex_hot, h_pick.at[sweep], h_picked.at[sweep])
        if more:
            h_buf[sweep + 1, me_t] = h_own
        else:
            h_last[...] = h_own
            h_store = pltpu.make_async_copy(h_last, h_out, local.at[6])
            h_store.start()
        if sweep > 0:
            arrive(w_come)
            get_rows(w_full, w_buf.at[sweep])
        stack_up(w_full)
        arrive(come)

        out, target = w_send.at[sweep], w_recv.at[sweep]
        send = sender("smp", sweep, out, target)
        part_of = functools.partial(part_of_picked, h_picked.at[sweep], h_part)
        come = slot_terms(part_of, (turned_high, turned_low), out, send)
        w_recv[sweep, me_s] = w_send[sweep, me_s]
        if more:
            mine = h_buf.at[sweep + 1, me_t]
            h_come = scatter("tex", phase + 1, lambda to: mine, mine)
        w_own = updated("smp", w_own, w_recv.at[sweep], smp_hot, come)
        if more:
            come = send_picked("smp", phase, w_own, smp_hot, w_pick.at[sweep], w_picked.at[sweep])
            w_buf[sweep + 1, me_s] = w_own
            arrive(come)
    w_last[...] = w_own
    w_store = pltpu.make_async_copy(w_last, w_out, local.at[7])
    w_store.start()
    for copy in started:
        copy.wait_send()
    h_store.wait()
    w_store.wait()


def per_device(n_tex, n_smp, blocks, observed, w_factor, h_factor):
    cap = blocks.shape[3]
    block = observed.shape[3]
    w_rows, texels = w_factor.shape
    h_rows, samples = h_factor.shape
    rank = w_rows * n_smp
    wide = cap * block + -(-cap * rank // LANES) * LANES
    phases = 2 + 4 * ITERS
    f32, half, vmem = jnp.float32, jnp.bfloat16, pltpu.VMEM
    dma = pltpu.SemaphoreType.DMA
    return pl.pallas_call(
        functools.partial(kernel, (n_tex, n_smp)),
        out_shape=(
            jax.ShapeDtypeStruct(w_factor.shape, f32),
            jax.ShapeDtypeStruct(h_factor.shape, f32),
        ),
        in_specs=[pl.BlockSpec(memory_space=pl.ANY)] * 4,
        out_specs=(pl.BlockSpec(memory_space=pl.ANY),) * 2,
        scratch_shapes=[
            pltpu.SMEM(blocks.shape[2:], jnp.int32),
            vmem((cap, block, block), f32),
            vmem((cap, block, block), half),
            vmem((cap, block, block), half),
            vmem((cap, block, block), half),
            vmem((cap, block, block), half),
            vmem((1, LANES), jnp.int32),
            vmem((n_tex, 1, LANES), jnp.int32),
            vmem((n_smp, 1, LANES), jnp.int32),
            pltpu.SMEM((n_tex, 1, LANES), jnp.int32),
            pltpu.SMEM((n_smp, 1, LANES), jnp.int32),
            pltpu.SMEM((n_tex * cap * (samples // block),), f32),
            pltpu.SMEM((n_smp * cap * (texels // block),), f32),
            vmem((ITERS, n_smp, w_rows, texels), f32),
            vmem((ITERS, n_tex, h_rows, samples), f32),
            vmem((rank, texels), f32),
            vmem((rank, samples), f32),
            vmem((ITERS, n_tex, h_rows, wide), f32),
            vmem((ITERS, n_tex, h_rows, wide), f32),
            vmem((ITERS, n_smp, w_rows, wide), f32),
            vmem((ITERS, n_smp, w_rows, wide), f32),
            vmem((ITERS, n_tex, h_rows, cap * block), f32),
            vmem((ITERS, n_tex, h_rows, cap * block), f32),
            vmem((ITERS, n_smp, w_rows, cap * block), f32),
            vmem((ITERS, n_smp, w_rows, cap * block), f32),
            vmem((rank, cap * block), f32),
            vmem((rank, cap * block), f32),
            vmem(h_factor.shape, f32),
            vmem(w_factor.shape, f32),
            vmem((3 * rank, max(texels, samples)), half),
            dma((phases, n_tex - 1)),
            dma((phases, n_tex - 1)),
            dma((phases, n_smp - 1)),
            dma((phases, n_smp - 1)),
            dma((8,)),
        ],
        compiler_params=pltpu.CompilerParams(
            collective_id=0, has_side_effects=True, vmem_limit_bytes=60 * 2**20
        ),
    )(
        blocks.reshape(blocks.shape[2:]),
        observed.reshape(cap, block, block),
        w_factor,
        h_factor,
    )


def solution(mesh):
    in_specs = (
        P("tex", "smp", None, None),
        P("tex", "smp", None, None),
        P("smp", "tex"),
        P("tex", "smp"),
    )
    out_specs = (P("smp", "tex"), P("tex", "smp"))
    return jax.shard_map(
        functools.partial(per_device, mesh.shape["tex"], mesh.shape["smp"]),
        mesh=mesh,
        in_specs=in_specs,
        out_specs=out_specs,
        check_vma=False,
    )
```

```python
import functools

import jax
import jax.numpy as jnp
from jax import lax
from jax.experimental import pallas as pl
from jax.experimental.pallas import tpu as pltpu
from jax.sharding import PartitionSpec as P

ITERS = 2
MESH = pl.DeviceIdType.MESH
LANES = 128
ROW_ROW = (((1,), (0,)), ((), ()))
LAST_LAST = (((1,), (1,)), ((), ()))


def halves(x):
    high = x.astype(jnp.bfloat16)
    low = (x - high.astype(jnp.float32)).astype(jnp.bfloat16)
    return high, low


def dot(a, b, dims=ROW_ROW):
    return lax.dot_general(a, b, dims, preferred_element_type=jnp.float32)


def weight(place, c):
    return (1 - jnp.minimum(jnp.abs(place - c), 1)).astype(jnp.float32)


def put_rows(buf, x, lanes):
    parts, rows, _ = buf.shape
    if rows % 8 == 0:
        buf[:, :, lanes] = x.reshape(parts, rows, x.shape[1])
    else:
        for p in range(parts):
            buf[p, :, lanes] = x[p * rows : (p + 1) * rows]


def get_rows(full, buf):
    parts, rows, _ = buf.shape
    for p in range(parts):
        full[p * rows : (p + 1) * rows, :] = buf[p]


def kernel(
    sizes, listing_hbm, values_hbm, w_in, h_in, w_out, h_out,
    listing, values, high, low, turned_high, turned_low,
    note, tex_note, smp_note, tex_list, smp_list, tex_hot, smp_hot,
    w_buf, h_buf, w_full, h_full, h_send, h_recv, w_send, w_recv,
    h_pick, h_picked, w_pick, w_picked, h_part, w_part, stack, stack_low,
    send_t, recv_t, send_s, recv_s, local,
):
    n_tex, n_smp = sizes
    cap, block, _ = values.shape
    rank, texels = w_full.shape
    samples = h_full.shape[1]
    me_t, me_s = lax.axis_index("tex"), lax.axis_index("smp")
    axes = {
        "tex": (me_t, n_tex, send_t, recv_t),
        "smp": (me_s, n_smp, send_s, recv_s),
    }

    fetch = [
        pltpu.make_async_copy(w_in, w_buf.at[0, me_s], local.at[0]),
        pltpu.make_async_copy(h_in, h_buf.at[0, me_t], local.at[1]),
        pltpu.make_async_copy(listing_hbm, listing, local.at[2]),
        pltpu.make_async_copy(values_hbm, values, local.at[3]),
    ]
    for copy in fetch:
        copy.start()

    barrier = pltpu.get_barrier_semaphore()
    for axis, (me, n, _, _) in axes.items():
        for d in range(1, n):
            pl.semaphore_signal(
                barrier, inc=1, device_id={axis: lax.rem(me + d, n)}, device_id_type=MESH
            )
    for copy in fetch[:3]:
        copy.wait()
    lane = lax.broadcasted_iota(jnp.int32, (1, LANES), 1)
    text = jnp.full((1, LANES), -1, jnp.int32)
    for side in range(2):
        for j in range(cap):
            text = jnp.where(lane == side * cap + j, listing[side, j], text)
    note[...] = text
    tex_note[me_t] = text
    smp_note[me_s] = text

    pl.semaphore_wait(barrier, n_tex + n_smp - 2)

    started = []

    def push(axis, phase, at, src, dst, to):
        _, _, send_sem, recv_sem = axes[axis]
        copy = pltpu.make_async_remote_copy(
            src_ref=src,
            dst_ref=dst,
            send_sem=send_sem.at[phase, at],
            recv_sem=recv_sem.at[phase, at],
            device_id={axis: to},
            device_id_type=MESH,
        )
        copy.start()
        started.append(copy)
        return copy

    def scatter(axis, phase, source_of, target):
        me, n, _, _ = axes[axis]
        copies = []
        for d in range(1, n):
            to = lax.rem(me + d, n)
            copies.append(push(axis, phase, d - 1, source_of(to), target, to))
        return copies

    def gather_begin(axis, phase, buf):
        me, n, _, _ = axes[axis]
        mine = buf.at[me]
        copies = []
        for d in range(1, n // 2):
            copies.append(push(axis, phase, d - 1, mine, mine, lax.rem(me + 2 * d, n)))
        mate = me + 1 - 2 * lax.rem(me, 2)
        copies.append(push(axis, phase, n // 2 - 1, mine, mine, mate))
        return copies

    def gather_forward(axis, phase, buf, copies):
        me, n, _, _ = axes[axis]
        mate = me + 1 - 2 * lax.rem(me, 2)
        late = copies[-1:]
        for d in range(1, n // 2):
            copies[d - 1].wait_recv()
            came = buf.at[lax.rem(me + n - 2 * d, n)]
            late.append(push(axis, phase, n // 2 - 1 + d, came, came, mate))
        return late

    def arrive(copies):
        for copy in copies:
            copy.wait_recv()

    w_come = gather_begin("smp", 0, w_buf.at[0])
    h_come = gather_begin("tex", 0, h_buf.at[0])
    notes = scatter("smp", 1, lambda to: note, smp_note.at[me_s])
    notes += scatter("tex", 1, lambda to: note, tex_note.at[me_t])

    h_come = gather_forward("tex", 0, h_buf.at[0], h_come)
    w_come = gather_forward("smp", 0, w_buf.at[0], w_come)
    arrive(notes)
    copies = [
        pltpu.make_async_copy(tex_note, tex_list, local.at[4]),
        pltpu.make_async_copy(smp_note, smp_list, local.at[5]),
    ]
    for copy in copies:
        copy.start()
    fetch[3].wait()
    for j in range(cap):
        high[j], low[j] = halves(values[j])
        turned_high[j], turned_low[j] = halves(values[j].T)
    arrive(w_come)
    get_rows(w_full, w_buf.at[0])

    def part_of_full(full, side, j):
        part = None
        for c in range(full.shape[1] // block):
            term = weight(listing[side, j], c) * full[:, c * block : (c + 1) * block]
            part = term if part is None else part + term
        return part

    def part_of_picked(picked, spare, j):
        where = slice(j * block, (j + 1) * block)
        if picked.shape[1] % 8 == 0:
            return picked[:, :, where].reshape(rank, block)
        if j == 0:
            get_rows(spare, picked)
        return spare[:, where]

    def slot_terms(part_of, weights, out, send):
        parts = []
        edge = cap * block
        for j in range(cap):
            parts.append(halves(part_of(j)))
            both = jnp.concatenate(parts[j], axis=0)
            twice = dot(both, weights[0][j])
            upper = twice[:rank] + (twice[rank:] + dot(parts[j][0], weights[1][j]))
            put_rows(out, upper, slice(j * block, (j + 1) * block))
            if j == cap - 2:
                come = send(0, pl.ds(0, edge - block))
        left = jnp.concatenate([half for pair in parts for half in pair], axis=0)
        right = jnp.concatenate([pair[0] for pair in parts] + [pair[1] for pair in parts], axis=0)
        every = dot(left, right, LAST_LAST)
        span = cap * rank
        gram = None
        for j in range(cap):
            top = every[2 * j * rank : (2 * j + 1) * rank]
            bottom = every[(2 * j + 1) * rank : (2 * j + 2) * rank]
            own = top[:, :span] + (top[:, span:] + bottom[:, :span])
            gram = own if gram is None else jnp.where(slot_of(rank) == j, own, gram)
        put_rows(out, gram, slice(edge, edge + span))
        return come + send(1, pl.ds(edge - block, out.shape[2] - edge + block))

    def slot_of(rows):
        return lax.broadcasted_iota(jnp.int32, (rows, cap * rank), 1) // rank

    def stack_up(full):
        part = halves(full[...])
        width = full.shape[1]
        for i in range(2 * cap):
            stack[i * rank : (i + 1) * rank, :width] = part[0]
        for i in range(cap):
            stack_low[i * rank : (i + 1) * rank, :width] = part[1]

    def updated(axis, own, recv, hot, come):
        me, n, _, _ = axes[axis]
        count = own.shape[1] // block
        upper, gram = [None] * count, [None] * count
        slots = slot_of(recv.shape[1])
        for d in range(n):
            p = lax.rem(me + n - d, n)
            if d > 0:
                arrive([come[d - 1], come[n - 1 + d - 1]])
            g = recv[p, :, cap * block : cap * block + cap * rank]
            for c in range(count):
                mixed = None
                for j in range(cap):
                    hit = hot[(p * cap + j) * count + c]
                    u = hit * recv[p, :, j * block : (j + 1) * block]
                    upper[c] = u if upper[c] is None else upper[c] + u
                    mixed = hit if mixed is None else jnp.where(slots == j, hit, mixed)
                gram[c] = mixed * g if gram[c] is None else gram[c] + mixed * g
        new = []
        for c in range(count):
            where = slice(c * block, (c + 1) * block)
            g_high, g_low = halves(gram[c])
            lower = dot(jnp.concatenate([g_high, g_low], axis=1), stack[:, where])
            lower = lower + dot(g_high, stack_low[:, where])
            new.append(own[:, where] * upper[c] / lower)
        return jnp.concatenate(new, axis=1)

    def send_picked(axis, phase, new, hot, pick, picked):
        me, n, _, _ = axes[axis]
        count = new.shape[1] // block
        copies = []
        for d in list(range(1, n)) + [0]:
            to = lax.rem(me + d, n)
            for j in range(cap):
                part = None
                for c in range(count):
                    hit = hot[(to * cap + j) * count + c]
                    term = hit * new[:, c * block : (c + 1) * block]
                    part = term if part is None else part + term
                (pick if d else picked)[to, :, j * block : (j + 1) * block] = part
            if d:
                copies.append(push(axis, phase, d - 1, pick.at[to], picked.at[me], to))
        return copies

    def sender(axis, sweep, out, target):
        me = axes[axis][0]

        def send(half, lanes):
            return scatter(
                axis, 2 + 4 * sweep + half,
                lambda to: out.at[to, :, lanes], target.at[me, :, lanes],
            )

        return send

    h_own, w_own = h_buf[0, me_t], w_buf[0, me_s]
    for sweep in range(ITERS):
        phase = 4 + 4 * sweep
        more = sweep < ITERS - 1
        out, target = h_send.at[sweep], h_recv.at[sweep]
        send = sender("tex", sweep, out, target)
        if sweep == 0:
            part_of = functools.partial(part_of_full, w_full, 0)
        else:
            part_of = functools.partial(part_of_picked, w_picked.at[sweep - 1], w_part)
        come = slot_terms(part_of, (high, low), out, send)
        h_recv[sweep, me_t] = h_send[sweep, me_t]
        if sweep == 0:
            for copy in copies:
                copy.wait()
            for lists, hot, n, side in ((tex_list, tex_hot, n_tex, 1), (smp_list, smp_hot, n_smp, 0)):
                count = (texels, samples)[side] // block
                for p in range(n):
                    for j in range(cap):
                        for c in range(count):
                            hot[(p * cap + j) * count + c] = weight(lists[p, 0, side * cap + j], c)
        else:
            mine = w_buf.at[sweep, me_s]
            w_come = scatter("smp", phase + 1, lambda to: mine, mine)
        arrive(h_come)
        get_rows(h_full, h_buf.at[sweep])
        stack_up(h_full)
        h_own = updated("tex", h_own, h_recv.at[sweep], tex_hot, come)
        come = send_picked("tex", phase, h_own, tex_hot, h_pick.at[sweep], h_picked.at[sweep])
        if more:
            h_buf[sweep + 1, me_t] = h_own
        else:
            h_out[...] = h_own
        if sweep > 0:
            arrive(w_come)
            get_rows(w_full, w_buf.at[sweep])
        stack_up(w_full)
        arrive(come)

        out, target = w_send.at[sweep], w_recv.at[sweep]
        send = sender("smp", sweep, out, target)
        part_of = functools.partial(part_of_picked, h_picked.at[sweep], h_part)
        come = slot_terms(part_of, (turned_high, turned_low), out, send)
        w_recv[sweep, me_s] = w_send[sweep, me_s]
        if more:
            mine = h_buf.at[sweep + 1, me_t]
            h_come = scatter("tex", phase + 1, lambda to: mine, mine)
        w_own = updated("smp", w_own, w_recv.at[sweep], smp_hot, come)
        if more:
            come = send_picked("smp", phase, w_own, smp_hot, w_pick.at[sweep], w_picked.at[sweep])
            w_buf[sweep + 1, me_s] = w_own
            arrive(come)
    w_out[...] = w_own
    for copy in started:
        copy.wait_send()


def per_device(n_tex, n_smp, blocks, observed, w_factor, h_factor):
    cap = blocks.shape[3]
    block = observed.shape[3]
    w_rows, texels = w_factor.shape
    h_rows, samples = h_factor.shape
    rank = w_rows * n_smp
    wide = cap * block + -(-cap * rank // LANES) * LANES
    phases = 2 + 4 * ITERS
    f32, half, vmem = jnp.float32, jnp.bfloat16, pltpu.VMEM
    dma = pltpu.SemaphoreType.DMA
    return pl.pallas_call(
        functools.partial(kernel, (n_tex, n_smp)),
        out_shape=(
            pltpu.VMEM(w_factor.shape, f32),
            pltpu.VMEM(h_factor.shape, f32),
        ),
        in_specs=[pl.BlockSpec(memory_space=pl.ANY)] * 4,
        out_specs=(pl.BlockSpec(memory_space=vmem),) * 2,
        scratch_shapes=[
            pltpu.SMEM(blocks.shape[2:], jnp.int32),
            vmem((cap, block, block), f32),
            vmem((cap, block, block), half),
            vmem((cap, block, block), half),
            vmem((cap, block, block), half),
            vmem((cap, block, block), half),
            vmem((1, LANES), jnp.int32),
            vmem((n_tex, 1, LANES), jnp.int32),
            vmem((n_smp, 1, LANES), jnp.int32),
            pltpu.SMEM((n_tex, 1, LANES), jnp.int32),
            pltpu.SMEM((n_smp, 1, LANES), jnp.int32),
            pltpu.SMEM((n_tex * cap * (samples // block),), f32),
            pltpu.SMEM((n_smp * cap * (texels // block),), f32),
            vmem((ITERS, n_smp, w_rows, texels), f32),
            vmem((ITERS, n_tex, h_rows, samples), f32),
            vmem((rank, texels), f32),
            vmem((rank, samples), f32),
            vmem((ITERS, n_tex, h_rows, wide), f32),
            vmem((ITERS, n_tex, h_rows, wide), f32),
            vmem((ITERS, n_smp, w_rows, wide), f32),
            vmem((ITERS, n_smp, w_rows, wide), f32),
            vmem((ITERS, n_tex, h_rows, cap * block), f32),
            vmem((ITERS, n_tex, h_rows, cap * block), f32),
            vmem((ITERS, n_smp, w_rows, cap * block), f32),
            vmem((ITERS, n_smp, w_rows, cap * block), f32),
            vmem((rank, cap * block), f32),
            vmem((rank, cap * block), f32),
            vmem((2 * cap * rank, max(texels, samples)), half),
            vmem((cap * rank, max(texels, samples)), half),
            dma((phases, n_tex - 1)),
            dma((phases, n_tex - 1)),
            dma((phases, n_smp - 1)),
            dma((phases, n_smp - 1)),
            dma((6,)),
        ],
        compiler_params=pltpu.CompilerParams(
            collective_id=0, has_side_effects=True, vmem_limit_bytes=60 * 2**20
        ),
    )(
        blocks.reshape(blocks.shape[2:]),
        observed.reshape(cap, block, block),
        w_factor,
        h_factor,
    )


def solution(mesh):
    in_specs = (
        P("tex", "smp", None, None),
        P("tex", "smp", None, None),
        P("smp", "tex"),
        P("tex", "smp"),
    )
    out_specs = (P("smp", "tex"), P("tex", "smp"))
    return jax.shard_map(
        functools.partial(per_device, mesh.shape["tex"], mesh.shape["smp"]),
        mesh=mesh,
        in_specs=in_specs,
        out_specs=out_specs,
        check_vma=False,
    )
```

```python
import functools

import jax
import jax.numpy as jnp
from jax import lax
from jax.experimental import pallas as pl
from jax.experimental.pallas import tpu as pltpu
from jax.sharding import PartitionSpec as P

ITERS = 2
MESH = pl.DeviceIdType.MESH
LANES = 128
ROW_ROW = (((1,), (0,)), ((), ()))
LAST_LAST = (((1,), (1,)), ((), ()))


def halves(x):
    high = x.astype(jnp.bfloat16)
    low = (x - high.astype(jnp.float32)).astype(jnp.bfloat16)
    return high, low


def dot(a, b, dims=ROW_ROW):
    return lax.dot_general(a, b, dims, preferred_element_type=jnp.float32)


def weight(place, c):
    return (1 - jnp.minimum(jnp.abs(place - c), 1)).astype(jnp.float32)


def put_rows(buf, x, lanes):
    parts, rows, _ = buf.shape
    if rows % 8 == 0:
        buf[:, :, lanes] = x.reshape(parts, rows, x.shape[1])
    else:
        for p in range(parts):
            buf[p, :, lanes] = x[p * rows : (p + 1) * rows]


def get_rows(full, buf):
    parts, rows, _ = buf.shape
    for p in range(parts):
        full[p * rows : (p + 1) * rows, :] = buf[p]


def kernel(
    sizes, listing_hbm, values_hbm, w_in, h_in, w_out, h_out,
    listing, values, high, low, turned_high, turned_low,
    note, tex_note, smp_note, tex_list, smp_list, tex_hot, smp_hot,
    w_buf, h_buf, w_full, h_full, h_send, h_recv, w_send, w_recv,
    h_pick, h_picked, w_pick, w_picked, h_part, w_part, stack, stack_low,
    send_t, recv_t, send_s, recv_s, local,
):
    n_tex, n_smp = sizes
    cap, block, _ = values.shape
    rank, texels = w_full.shape
    samples = h_full.shape[1]
    me_t, me_s = lax.axis_index("tex"), lax.axis_index("smp")
    axes = {
        "tex": (me_t, n_tex, send_t, recv_t),
        "smp": (me_s, n_smp, send_s, recv_s),
    }

    fetch = [
        pltpu.make_async_copy(w_in, w_buf.at[0, me_s], local.at[0]),
        pltpu.make_async_copy(h_in, h_buf.at[0, me_t], local.at[1]),
        pltpu.make_async_copy(listing_hbm, listing, local.at[2]),
        pltpu.make_async_copy(values_hbm, values, local.at[3]),
    ]
    for copy in fetch:
        copy.start()

    barrier = pltpu.get_barrier_semaphore()
    for axis, (me, n, _, _) in axes.items():
        for d in range(1, n):
            pl.semaphore_signal(
                barrier, inc=1, device_id={axis: lax.rem(me + d, n)}, device_id_type=MESH
            )
    for copy in fetch[:3]:
        copy.wait()
    lane = lax.broadcasted_iota(jnp.int32, (1, LANES), 1)
    text = jnp.full((1, LANES), -1, jnp.int32)
    for side in range(2):
        for j in range(cap):
            text = jnp.where(lane == side * cap + j, listing[side, j], text)
    note[...] = text
    tex_note[me_t] = text
    smp_note[me_s] = text

    pl.semaphore_wait(barrier, n_tex + n_smp - 2)

    started = []

    def push(axis, phase, at, src, dst, to):
        _, _, send_sem, recv_sem = axes[axis]
        copy = pltpu.make_async_remote_copy(
            src_ref=src,
            dst_ref=dst,
            send_sem=send_sem.at[phase, at],
            recv_sem=recv_sem.at[phase, at],
            device_id={axis: to},
            device_id_type=MESH,
        )
        copy.start()
        started.append(copy)
        return copy

    def scatter(axis, phase, source_of, target):
        me, n, _, _ = axes[axis]
        copies = []
        for d in range(1, n):
            to = lax.rem(me + d, n)
            copies.append(push(axis, phase, d - 1, source_of(to), target, to))
        return copies

    def gather_begin(axis, phase, buf):
        me, n, _, _ = axes[axis]
        mine = buf.at[me]
        copies = []
        for d in range(1, n // 2):
            copies.append(push(axis, phase, d - 1, mine, mine, lax.rem(me + 2 * d, n)))
        mate = me + 1 - 2 * lax.rem(me, 2)
        copies.append(push(axis, phase, n // 2 - 1, mine, mine, mate))
        return copies

    def gather_forward(axis, phase, buf, copies):
        me, n, _, _ = axes[axis]
        mate = me + 1 - 2 * lax.rem(me, 2)
        late = copies[-1:]
        for d in range(1, n // 2):
            copies[d - 1].wait_recv()
            came = buf.at[lax.rem(me + n - 2 * d, n)]
            late.append(push(axis, phase, n // 2 - 1 + d, came, came, mate))
        return late

    def arrive(copies):
        for copy in copies:
            copy.wait_recv()

    w_come = gather_begin("smp", 0, w_buf.at[0])
    h_come = gather_begin("tex", 0, h_buf.at[0])
    notes = scatter("smp", 1, lambda to: note, smp_note.at[me_s])
    notes += scatter("tex", 1, lambda to: note, tex_note.at[me_t])

    fetch[3].wait()
    for j in range(cap):
        high[j], low[j] = halves(values[j])
        turned_high[j], turned_low[j] = halves(values[j].T)
    h_come = gather_forward("tex", 0, h_buf.at[0], h_come)
    w_come = gather_forward("smp", 0, w_buf.at[0], w_come)
    arrive(notes)
    copies = [
        pltpu.make_async_copy(tex_note, tex_list, local.at[4]),
        pltpu.make_async_copy(smp_note, smp_list, local.at[5]),
    ]
    for copy in copies:
        copy.start()
    arrive(w_come)
    get_rows(w_full, w_buf.at[0])

    def part_of_full(full, side, j):
        part = None
        for c in range(full.shape[1] // block):
            term = weight(listing[side, j], c) * full[:, c * block : (c + 1) * block]
            part = term if part is None else part + term
        return part

    def part_of_picked(picked, spare, j):
        where = slice(j * block, (j + 1) * block)
        if picked.shape[1] % 8 == 0:
            return picked[:, :, where].reshape(rank, block)
        if j == 0:
            get_rows(spare, picked)
        return spare[:, where]

    def slot_terms(part_of, weights, out, send):
        parts = []
        edge = cap * block
        for j in range(cap):
            parts.append(halves(part_of(j)))
            both = jnp.concatenate(parts[j], axis=0)
            twice = dot(both, weights[0][j])
            upper = twice[:rank] + (twice[rank:] + dot(parts[j][0], weights[1][j]))
            put_rows(out, upper, slice(j * block, (j + 1) * block))
            if j == cap - 2:
                come = send(0, pl.ds(0, edge - block))
        left = jnp.concatenate([half for pair in parts for half in pair], axis=0)
        right = jnp.concatenate([pair[0] for pair in parts] + [pair[1] for pair in parts], axis=0)
        every = dot(left, right, LAST_LAST)
        span = cap * rank
        gram = None
        for j in range(cap):
            top = every[2 * j * rank : (2 * j + 1) * rank]
            bottom = every[(2 * j + 1) * rank : (2 * j + 2) * rank]
            own = top[:, :span] + (top[:, span:] + bottom[:, :span])
            gram = own if gram is None else jnp.where(slot_of(rank) == j, own, gram)
        put_rows(out, gram, slice(edge, edge + span))
        return come + send(1, pl.ds(edge - block, out.shape[2] - edge + block))

    def slot_of(rows):
        return lax.broadcasted_iota(jnp.int32, (rows, cap * rank), 1) // rank

    def stack_up(full):
        part = halves(full[...])
        width = full.shape[1]
        for i in range(2 * cap):
            stack[i * rank : (i + 1) * rank, :width] = part[0]
        for i in range(cap):
            stack_low[i * rank : (i + 1) * rank, :width] = part[1]

    def updated(axis, own, recv, hot, come):
        me, n, _, _ = axes[axis]
        count = own.shape[1] // block
        upper, gram = [None] * count, [None] * count
        slots = slot_of(recv.shape[1])
        for d in range(n):
            p = lax.rem(me + n - d, n)
            if d > 0:
                arrive([come[d - 1], come[n - 1 + d - 1]])
            g = recv[p, :, cap * block : cap * block + cap * rank]
            for c in range(count):
                mixed = None
                for j in range(cap):
                    hit = hot[(p * cap + j) * count + c]
                    u = hit * recv[p, :, j * block : (j + 1) * block]
                    upper[c] = u if upper[c] is None else upper[c] + u
                    mixed = hit if mixed is None else jnp.where(slots == j, hit, mixed)
                gram[c] = mixed * g if gram[c] is None else gram[c] + mixed * g
        new = []
        for c in range(count):
            where = slice(c * block, (c + 1) * block)
            g_high, g_low = halves(gram[c])
            lower = dot(jnp.concatenate([g_high, g_low], axis=1), stack[:, where])
            lower = lower + dot(g_high, stack_low[:, where])
            new.append(own[:, where] * upper[c] / lower)
        return jnp.concatenate(new, axis=1)

    def send_picked(axis, phase, new, hot, pick, picked):
        me, n, _, _ = axes[axis]
        count = new.shape[1] // block
        copies = []
        for d in list(range(1, n)) + [0]:
            to = lax.rem(me + d, n)
            for j in range(cap):
                part = None
                for c in range(count):
                    hit = hot[(to * cap + j) * count + c]
                    term = hit * new[:, c * block : (c + 1) * block]
                    part = term if part is None else part + term
                (pick if d else picked)[to, :, j * block : (j + 1) * block] = part
            if d:
                copies.append(push(axis, phase, d - 1, pick.at[to], picked.at[me], to))
        return copies

    def sender(axis, sweep, out, target):
        me = axes[axis][0]

        def send(half, lanes):
            return scatter(
                axis, 2 + 4 * sweep + half,
                lambda to: out.at[to, :, lanes], target.at[me, :, lanes],
            )

        return send

    h_own, w_own = h_buf[0, me_t], w_buf[0, me_s]
    for sweep in range(ITERS):
        phase = 4 + 4 * sweep
        more = sweep < ITERS - 1
        out, target = h_send.at[sweep], h_recv.at[sweep]
        send = sender("tex", sweep, out, target)
        if sweep == 0:
            part_of = functools.partial(part_of_full, w_full, 0)
        else:
            part_of = functools.partial(part_of_picked, w_picked.at[sweep - 1], w_part)
        come = slot_terms(part_of, (high, low), out, send)
        h_recv[sweep, me_t] = h_send[sweep, me_t]
        if sweep == 0:
            for copy in copies:
                copy.wait()
            for lists, hot, n, side in ((tex_list, tex_hot, n_tex, 1), (smp_list, smp_hot, n_smp, 0)):
                count = (texels, samples)[side] // block
                for p in range(n):
                    for j in range(cap):
                        for c in range(count):
                            hot[(p * cap + j) * count + c] = weight(lists[p, 0, side * cap + j], c)
        else:
            mine = w_buf.at[sweep, me_s]
            w_come = scatter("smp", phase + 1, lambda to: mine, mine)
        arrive(h_come)
        get_rows(h_full, h_buf.at[sweep])
        stack_up(h_full)
        h_own = updated("tex", h_own, h_recv.at[sweep], tex_hot, come)
        come = send_picked("tex", phase, h_own, tex_hot, h_pick.at[sweep], h_picked.at[sweep])
        if more:
            h_buf[sweep + 1, me_t] = h_own
        else:
            h_out[...] = h_own
        if sweep > 0:
            arrive(w_come)
            get_rows(w_full, w_buf.at[sweep])
        stack_up(w_full)
        arrive(come)

        out, target = w_send.at[sweep], w_recv.at[sweep]
        send = sender("smp", sweep, out, target)
        part_of = functools.partial(part_of_picked, h_picked.at[sweep], h_part)
        come = slot_terms(part_of, (turned_high, turned_low), out, send)
        w_recv[sweep, me_s] = w_send[sweep, me_s]
        if more:
            mine = h_buf.at[sweep + 1, me_t]
            h_come = scatter("tex", phase + 1, lambda to: mine, mine)
        w_own = updated("smp", w_own, w_recv.at[sweep], smp_hot, come)
        if more:
            come = send_picked("smp", phase, w_own, smp_hot, w_pick.at[sweep], w_picked.at[sweep])
            w_buf[sweep + 1, me_s] = w_own
            arrive(come)
    w_out[...] = w_own
    for copy in started:
        copy.wait_send()


def per_device(n_tex, n_smp, blocks, observed, w_factor, h_factor):
    cap = blocks.shape[3]
    block = observed.shape[3]
    w_rows, texels = w_factor.shape
    h_rows, samples = h_factor.shape
    rank = w_rows * n_smp
    wide = cap * block + -(-cap * rank // LANES) * LANES
    phases = 2 + 4 * ITERS
    f32, half, vmem = jnp.float32, jnp.bfloat16, pltpu.VMEM
    dma = pltpu.SemaphoreType.DMA
    return pl.pallas_call(
        functools.partial(kernel, (n_tex, n_smp)),
        out_shape=(
            pltpu.VMEM(w_factor.shape, f32),
            pltpu.VMEM(h_factor.shape, f32),
        ),
        in_specs=[pl.BlockSpec(memory_space=pl.ANY)] * 4,
        out_specs=(pl.BlockSpec(memory_space=vmem),) * 2,
        scratch_shapes=[
            pltpu.SMEM(blocks.shape[2:], jnp.int32),
            vmem((cap, block, block), f32),
            vmem((cap, block, block), half),
            vmem((cap, block, block), half),
            vmem((cap, block, block), half),
            vmem((cap, block, block), half),
            vmem((1, LANES), jnp.int32),
            vmem((n_tex, 1, LANES), jnp.int32),
            vmem((n_smp, 1, LANES), jnp.int32),
            pltpu.SMEM((n_tex, 1, LANES), jnp.int32),
            pltpu.SMEM((n_smp, 1, LANES), jnp.int32),
            pltpu.SMEM((n_tex * cap * (samples // block),), f32),
            pltpu.SMEM((n_smp * cap * (texels // block),), f32),
            vmem((ITERS, n_smp, w_rows, texels), f32),
            vmem((ITERS, n_tex, h_rows, samples), f32),
            vmem((rank, texels), f32),
            vmem((rank, samples), f32),
            vmem((ITERS, n_tex, h_rows, wide), f32),
            vmem((ITERS, n_tex, h_rows, wide), f32),
            vmem((ITERS, n_smp, w_rows, wide), f32),
            vmem((ITERS, n_smp, w_rows, wide), f32),
            vmem((ITERS, n_tex, h_rows, cap * block), f32),
            vmem((ITERS, n_tex, h_rows, cap * block), f32),
            vmem((ITERS, n_smp, w_rows, cap * block), f32),
            vmem((ITERS, n_smp, w_rows, cap * block), f32),
            vmem((rank, cap * block), f32),
            vmem((rank, cap * block), f32),
            vmem((2 * cap * rank, max(texels, samples)), half),
            vmem((cap * rank, max(texels, samples)), half),
            dma((phases, n_tex - 1)),
            dma((phases, n_tex - 1)),
            dma((phases, n_smp - 1)),
            dma((phases, n_smp - 1)),
            dma((6,)),
        ],
        compiler_params=pltpu.CompilerParams(
            collective_id=0, has_side_effects=True, vmem_limit_bytes=60 * 2**20
        ),
    )(
        blocks.reshape(blocks.shape[2:]),
        observed.reshape(cap, block, block),
        w_factor,
        h_factor,
    )


def solution(mesh):
    in_specs = (
        P("tex", "smp", None, None),
        P("tex", "smp", None, None),
        P("smp", "tex"),
        P("tex", "smp"),
    )
    out_specs = (P("smp", "tex"), P("tex", "smp"))
    return jax.shard_map(
        functools.partial(per_device, mesh.shape["tex"], mesh.shape["smp"]),
        mesh=mesh,
        in_specs=in_specs,
        out_specs=out_specs,
        check_vma=False,
    )
```
